512 devices in a mesh: gx: 8 (over y), gy: 4 (over z_lo), gz: 16 (over z_hi, x, core).
Axes of the slice: x: 4, y: 8, z: 8 (z_hi: 2, z_lo: 4; z = z_hi * 4 + z_lo), core: 2. Of those that a mesh axis runs over, the one named last changes fastest.
Arguments:
- field: float32 [1024, 8, 32, 512], P('gx', None, 'gz', 'gy'), may hold values from -72 to 72
- factor_one: float32 [1024, 256], P('gx'), may hold values from -0.25 to 0.25
- factor_two: float32 [512, 128], P('gy'), may hold values from -0.375 to 0.375
Outputs:
- gram_one: float32 [1024, 1024], P('gx', ('gy', 'gz'))
- gram_two: float32 [512, 512], P('gy')
- core: float32 [256, 8, 32, 128], P('gx', None, 'gz', 'gy')
The draws below stay inside these ranges and needn't reach their ends.
All inputs are finite; a program needn't handle non-finite values.
Results may differ from the reference program's by a relative error of at most 0.000078.
Values sent between devices are 32-bit elements; how exact they have to be, the bound alone decides.
No kernel may reach another device: no remote copies, remote signals or barrier semaphores. Data moves between devices by JAX's collectives and lax.ppermute only.
A program may use at most 64 MiB of HBM per device.

```python
import jax
import jax.numpy as jnp
from jax import lax

I1 = 1024
I2 = 512
R1 = 256
R2 = 128
TL = 8
I3 = 32


def draw_field(key, part):
    key = jax.random.fold_in(key, 11)
    key_row, key_slab, key_col, key_base = jax.random.split(key, 4)
    row_scale = jnp.exp(jax.random.uniform(key_row, (I1, 1, 1, 1), jnp.float32, jnp.log(0.3), jnp.log(3.0)))
    slab_scale = jnp.exp(jax.random.uniform(key_slab, (1, TL, I3, 1), jnp.float32, jnp.log(0.5), jnp.log(2.0)))
    col_scale = jnp.exp(jax.random.uniform(key_col, (1, 1, 1, I2), jnp.float32, jnp.log(0.5), jnp.log(2.0)))
    base = jax.random.normal(key_base, (I1, TL, I3, I2), jnp.float32)
    base = jnp.clip(base, -6.0, 6.0)
    return (base * row_scale * slab_scale * col_scale).astype(jnp.float32)


def strengthened(entries, key, source, target, shards_of, factor):
    def block_of(position):
        return (jnp.arange(entries.shape[position]) // (entries.shape[position] // shards_of)).reshape((-1,) + (1,) * (entries.ndim - 1 - position))

    near = jax.random.permutation(key, shards_of)[block_of(target)]
    other_side = (block_of(target) + shards_of // 2) % shards_of
    return jnp.where((block_of(source) == near) | (block_of(source) == other_side), factor * entries, entries)


def block_levels(rng, shape, cuts, smallest, largest):
    factor_of, own = 1.0, jax.random.fold_in(rng, 6)
    for dim, shards_of in cuts:
        draws = jnp.exp(jax.random.uniform(jax.random.fold_in(own, dim), (shards_of,), jnp.float32, smallest / len(cuts), largest / len(cuts)))
        factor_of = factor_of * jnp.repeat(draws, shape[dim] // shards_of).reshape([-1 if axis == dim else 1 for axis in range(len(shape))])
    return factor_of


def noise_with(key, extent, scale, reach, cuts, heavy, kind=jnp.bfloat16):
    values = scale * jax.random.normal(key, extent, jnp.float32)
    if cuts:
        values = values * block_levels(key, extent, cuts, -0.22, 0.18)
    return jnp.clip(strengthened(values, jax.random.fold_in(key, 3), *heavy), -reach, reach).astype(kind)


def setup_inputs(seed: int = 0) -> dict:
    key_list = jax.random.split(jax.random.key(seed), 4)
    field = draw_field(jax.random.fold_in(key_list[3], 71), 0)
    factor_one = noise_with(key_list[1], (I1, R1), I1 ** -0.5, 0.25, ((0, 8),), (0, 1, 8, 2.0), jnp.float32)
    factor_two = noise_with(key_list[2], (I2, R2), I2 ** -0.5, 0.375, ((0, 4),), (0, 1, 4, 2.0), jnp.float32)
    return {"field": field, "factor_one": factor_one, "factor_two": factor_two}


def reference(field, factor_one, factor_two):
    highest = lax.Precision.HIGHEST
    field_rows = field.reshape(I1, -1)
    gram_one = jnp.dot(field_rows, field_rows.T, precision=highest) / (I2 * I3 * TL)
    projected = jnp.dot(factor_one.T, field_rows, precision=highest).reshape(R1, TL, I3, I2)
    gram_two = jnp.tensordot(projected, projected, axes=([0, 1, 2], [0, 1, 2]), precision=highest) / (R1 * I3 * TL)
    core = jnp.tensordot(projected, factor_two, axes=([3], [0]), precision=highest)
    return gram_one, gram_two, core
```

```python
import jax
import jax.numpy as jnp
from jax import lax
from jax.sharding import Mesh
from jax.sharding import PartitionSpec as P

NY, NZL, NZH, NX, NC = 8, 4, 2, 4, 2
PREC = lax.Precision.HIGH


def exchange(a, axes):
    return lax.all_to_all(a, axes, 0, 0)


def per_device(field, u, v):
    f32 = jnp.float32
    core_id = lax.axis_index("c")

    f = jnp.transpose(field, (1, 2, 0, 3))
    f = exchange(f, "y")
    u_all = lax.all_gather(u, "y", axis=0)

    z = lax.dot_general(
        jnp.transpose(f, (1, 0, 2, 3)).reshape(2, 1024, 128),
        u_all.reshape(1024, 256),
        (((1,), (0,)), ((), ())),
        precision=PREC,
        preferred_element_type=f32,
    )
    z = jnp.transpose(z, (0, 2, 1)).reshape(512, 128)

    vt = jnp.transpose(v).reshape(NZL, 32, 128)
    zv = jnp.concatenate([jnp.broadcast_to(z, (NZL, 512, 128)), vt], axis=1)
    zv = exchange(zv, "zl")
    zg, vg = zv[:, :512], zv[:, 512:]

    g2 = lax.dot_general(
        z, jnp.transpose(zg, (1, 0, 2)).reshape(512, 512), (((0,), (0,)), ((), ())),
        precision=PREC, preferred_element_type=f32,
    )

    zr = zg.reshape(NZL, 2, 8, 4, 8, 128)
    zr = jnp.transpose(zr, (2, 1, 4, 3, 0, 5)).reshape(128, 4 * 512)
    vd = jnp.eye(4, dtype=f32)[:, None, :, None, None] * jnp.transpose(vg, (1, 0, 2))[None, :, None]
    vd = vd.reshape(128, 4 * 512)
    core_rows = lax.dot_general(
        zr, vd, (((1,), (1,)), ((), ())), precision=PREC, preferred_element_type=f32
    )

    other = lax.ppermute(f, "c", [(0, 1), (1, 0)])

    def rows_of(a):
        return jnp.transpose(a, (0, 2, 1, 3)).reshape(1024, 256)

    cells = jnp.concatenate([rows_of(f), rows_of(other)], axis=1)
    mine = cells.reshape(8, 4, 2, 16, 512)
    mine = lax.dynamic_index_in_dim(mine, core_id, 2, keepdims=False)
    mine = jnp.transpose(mine, (1, 0, 2, 3)).reshape(512, 512)
    g1 = lax.dot_general(
        mine, cells, (((1,), (1,)), ((), ())), precision=PREC, preferred_element_type=f32
    ).reshape(NX, 128, 1024)
    g1 = jnp.sum(exchange(g1, "x"), axis=0)
    g1 = jnp.transpose(g1.reshape(128, 8, 128), (1, 0, 2))

    g2 = jnp.sum(exchange(g2.reshape(8, 16, 512), ("x", "c")), axis=0)
    g2 = jnp.transpose(g2.reshape(16, 4, 128), (1, 0, 2)).reshape(64, 128)

    send = jnp.concatenate(
        [g1, core_rows.reshape(8, 16, 128), jnp.broadcast_to(g2, (8, 64, 128))], axis=1
    )
    got = exchange(send, "y")
    g1 = jnp.sum(got[:, :128], axis=0)
    core = got[:, 128:144].reshape(8, 2, 8, 4, 32)
    core = jnp.transpose(core, (3, 2, 0, 1, 4)).reshape(32, 8, 2, 32)
    g2 = jnp.sum(got[:, 144:], axis=0)
    g2 = g2 + lax.ppermute(g2, "zh", [(0, 1), (1, 0)])
    g2 = exchange(jnp.broadcast_to(g2, (8, 64, 128)), ("x", "c"))
    g2 = jnp.transpose(g2.reshape(8, 4, 16, 128), (0, 2, 1, 3)).reshape(128, 512)
    gram_two = g2 / 65536.0

    g1 = jnp.sum(exchange(g1.reshape(8, 16, 128), ("zl", "zh")), axis=0)
    gram_one = jnp.transpose(g1) / 131072.0
    return gram_one, gram_two, core


def solution(mesh):
    split = Mesh(mesh.devices.reshape(NY, NZL, NZH, NX, NC), ("y", "zl", "zh", "x", "c"))
    gz = ("zh", "x", "c")
    return jax.shard_map(
        per_device,
        mesh=split,
        in_specs=(P("y", None, gz, "zl"), P("y", None), P("zl", None)),
        out_specs=(P("y", ("zl",) + gz), P("zl", None), P("y", None, gz, "zl")),
        check_vma=False,
    )
```

```python
import jax
import jax.numpy as jnp
from jax import lax
from jax.sharding import Mesh
from jax.sharding import PartitionSpec as P

NY, NZL, NZH, NX, NC = 8, 4, 2, 4, 2
PREC = lax.Precision.HIGH


def exchange(a, axes):
    return lax.all_to_all(a, axes, 0, 0)


def dot(a, b, dims):
    return lax.dot_general(a, b, (dims, ((), ())), precision=PREC, preferred_element_type=jnp.float32)


def per_device(field, u, v):
    f32 = jnp.float32
    core_id = lax.axis_index("c")
    x_id = lax.axis_index("x")

    u_half = lax.dynamic_slice_in_dim(u, 128 * core_id, 128, 1)
    send = jnp.concatenate(
        [jnp.transpose(field, (1, 2, 0, 3)), jnp.broadcast_to(u_half, (NY, 1, 128, 128))], axis=1
    )
    own = exchange(send, "y")
    other = lax.ppermute(own, "c", [(0, 1), (1, 0)])

    f = own[:, :2]
    z = jnp.concatenate(
        [dot(own[:, 2], f, ((0, 1), (0, 2))), dot(other[:, 2], f, ((0, 1), (0, 2)))], axis=0
    ).reshape(512, 128)

    vt = jnp.transpose(v).reshape(NZL, 32, 128)
    zv = jnp.concatenate([jnp.broadcast_to(z, (NZL, 512, 128)), vt], axis=1)
    zv = exchange(zv, "zl")
    zg, vg = zv[:, :512], zv[:, 512:]

    def rows_of(a):
        return jnp.transpose(a[:, :2], (0, 2, 1, 3)).reshape(1024, 256)

    cells = jnp.concatenate([rows_of(own), rows_of(other)], axis=1)
    mine = cells.reshape(8, 4, 2, 16, 512)
    mine = lax.dynamic_index_in_dim(mine, core_id, 2, keepdims=False)
    mine = jnp.transpose(mine, (1, 0, 2, 3)).reshape(512, 512)
    g1 = dot(mine, cells, ((1,), (1,))).reshape(NX, 128, 1024)
    total = lax.dynamic_index_in_dim(g1, x_id, 0, keepdims=False)
    for d in (2, 1, 3):
        piece = lax.dynamic_index_in_dim(g1, (x_id + d) % NX, 0, keepdims=False)
        total = total + lax.ppermute(piece, "x", [(i, (i + d) % NX) for i in range(NX)])
    g1 = jnp.transpose(total.reshape(128, 8, 128), (1, 0, 2))

    g2 = dot(z, jnp.transpose(zg, (1, 0, 2)).reshape(512, 512), ((0,), (0,)))
    g2 = jnp.sum(exchange(g2.reshape(8, 16, 512), ("x", "c")), axis=0)
    g2 = jnp.transpose(g2.reshape(16, 4, 128), (1, 0, 2)).reshape(64, 128)

    zr = zg.reshape(NZL, 8, 4, 16, 128)
    zr = jnp.transpose(zr, (1, 3, 2, 0, 4)).reshape(128, 4 * 512)
    vd = jnp.eye(4, dtype=f32)[:, None, :, None, None] * jnp.transpose(vg, (1, 0, 2))[None, :, None]
    core_rows = dot(zr, vd.reshape(128, 4 * 512), ((1,), (1,))).reshape(8, 16, 128)
    core_rows = jnp.where(core_id == 0, core_rows, jnp.roll(core_rows, 4, axis=0))

    send = jnp.concatenate([g1, core_rows, jnp.broadcast_to(g2, (8, 64, 128))], axis=1)
    got = exchange(send, "y")
    core = got[:, 128:144].reshape(8, 8, 2, 4, 32)
    core = jnp.transpose(core, (3, 1, 0, 2, 4)).reshape(32, 8, 2, 32)
    g1 = jnp.sum(got[:, :128], axis=0).reshape(8, 16, 128)
    g2 = jnp.sum(got[:, 144:], axis=0)

    got = exchange(jnp.concatenate([g1, jnp.broadcast_to(g2, (8, 64, 128))], axis=1), ("zl", "zh"))
    gram_one = jnp.transpose(jnp.sum(got[:, :16], axis=0)) / 131072.0
    zl_id = lax.axis_index("zl")
    g2 = jnp.sum(lax.dynamic_slice_in_dim(got, 2 * zl_id, 2, 0)[:, 16:], axis=0)
    g2 = exchange(jnp.broadcast_to(g2, (8, 64, 128)), ("x", "c"))
    g2 = jnp.transpose(g2.reshape(8, 4, 16, 128), (0, 2, 1, 3)).reshape(128, 512)
    gram_two = g2 / 65536.0
    return gram_one, gram_two, core


def solution(mesh):
    split = Mesh(mesh.devices.reshape(NY, NZL, NZH, NX, NC), ("y", "zl", "zh", "x", "c"))
    gz = ("zh", "x", "c")
    return jax.shard_map(
        per_device,
        mesh=split,
        in_specs=(P("y", None, gz, "zl"), P("y", None), P("zl", None)),
        out_specs=(P("y", ("zl",) + gz), P("zl", None), P("y", None, gz, "zl")),
        check_vma=False,
    )
```

```python
import jax
import jax.numpy as jnp
from jax import lax
from jax.experimental import pallas as pl
from jax.experimental.pallas import tpu as pltpu
from jax.sharding import Mesh
from jax.sharding import PartitionSpec as P

NY, NYL, NZL, NZH, NX, NC = 8, 4, 4, 2, 4, 2
Y = ("yh", "yl")
F32, BF16 = jnp.float32, jnp.bfloat16


def exchange(a, axes):
    return lax.all_to_all(a, axes, 0, 0)


def shift(a, axis, size, d):
    return lax.ppermute(a, axis, [(i, (i + d) % size) for i in range(size)])


def split(a):
    hi = a.astype(BF16)
    return hi, (a - hi.astype(F32)).astype(BF16)


def dot3(a, b, dims):
    def one(p, q):
        return lax.dot_general(p, q, (dims, ((), ())), preferred_element_type=F32)

    return one(a[0], b[0]) + (one(a[0], b[1]) + one(a[1], b[0]))


def project_kernel(ids, own, other, after, o0, o1, o2, o3, res):
    c = ids[1]
    total = [jnp.zeros((128, 256), F32)] * 2
    for y in range(NY):
        f = split(jnp.concatenate([own[y, 0], own[y, 1]], axis=1))
        for h, ref in enumerate((own, other)):
            total[h] += dot3(split(ref[y, 2]), f, ((0,), (0,)))
    for h in range(2):
        half = c if h == 0 else 1 - c
        for rg in range(4):
            k, first = rg // 2, 4 * (rg % 2)
            at = pl.multiple_of(32 * rg + 16 * half, 16)
            for g in range(4):
                rows = [
                    total[h][32 * yq + 8 * g + first : 32 * yq + 8 * g + first + 4, 128 * k : 128 * k + 128]
                    for yq in range(4)
                ]
                res[g, pl.ds(at, 16), :] = jnp.concatenate(rows, axis=0)
    for d, o in enumerate((o0, o1, o2, o3)):
        o[...] = res[lax.rem(ids[2] + d, NZL)]


def gram_one_kernel(ids, own, other, out, hi, lo, row_hi, row_lo):
    n = pl.program_id(0)

    @pl.when(n == 0)
    def _():
        for i, ref in enumerate((own, other)):
            for k in range(2):
                for y in range(NY):
                    col = 256 * i + 128 * k
                    a, b = split(ref[y, k])
                    hi[128 * y : 128 * y + 128, col : col + 128] = a
                    lo[128 * y : 128 * y + 128, col : col + 128] = b
        for x in range(NX):
            for b in range(8):
                src = pl.ds(pl.multiple_of(128 * b + 32 * x + 16 * ids[1], 16), 16)
                dst = slice(128 * x + 16 * b, 128 * x + 16 * b + 16)
                row_hi[dst, :] = hi[src, :]
                row_lo[dst, :] = lo[src, :]

    cols = pl.ds(pl.multiple_of(256 * n, 256), 256)
    r = dot3((row_hi[...], row_lo[...]), (hi[cols, :], lo[cols, :]), ((1,), (1,)))
    for x in range(NX):
        for y in range(2):
            for b in range(8):
                at = 128 * x + 16 * b
                out[x, 8 * y + b] = r[at : at + 16, 128 * y : 128 * y + 128]


def gram_two_kernel(ids, own, other, o0, o1, o2, o3, hi, lo, res):
    for n, ref in enumerate((own, other)):
        for b in range(4):
            rows = slice(128 * n, 128 * n + 128)
            cols = pl.ds(pl.multiple_of(128 * lax.rem(ids[2] + NZL - b, NZL), 128), 128)
            p, q = split(ref[b])
            hi[rows, cols] = p
            lo[rows, cols] = q
    cols = pl.ds(pl.multiple_of(256 * ids[1], 256), 256)
    res[...] = dot3((hi[...], lo[...]), (hi[:, cols], lo[:, cols]), ((0,), (0,)))
    for d, o in enumerate((o0, o1, o2, o3)):
        x = lax.rem(ids[0] + d, NX)
        for zl in range(NZL):
            part = res[pl.ds(pl.multiple_of(128 * zl + 32 * x, 32), 32), :]
            for yl in range(NYL):
                for lb in range(2):
                    o[NZL * (NYL * lb + yl) + zl] = part[8 * yl : 8 * yl + 8, 128 * lb : 128 * lb + 128]


def core_kernel(ids, z, v0, v1, v2, v3, out):
    lane = lax.broadcasted_iota(jnp.int32, (128, 128), 1)
    total = jnp.zeros((32, 512), F32)
    for n, v in enumerate((v0, v1, v2, v3)):
        zn, vn = z[n], v[...]
        moved = [vn] + [pltpu.roll(vn, 32 * d, 1) for d in range(1, 4)]
        for rg in range(4):
            here = (lane >= 32 * rg) & (lane < 32 * rg + 32)
            cols = [jnp.where(here, moved[(rg - zl) % 4], 0.0) for zl in range(NZL)]
            total += dot3(split(zn[32 * rg : 32 * rg + 32]), split(jnp.concatenate(cols, axis=1)), ((1,), (0,)))
    for y in range(NY):
        for zl in range(NZL):
            part = total[4 * y : 4 * y + 4, 128 * zl : 128 * zl + 128]
            out[y, zl] = jnp.concatenate([part, part], axis=0)


def call(kernel, out_shape, flops, *args, scratch=(), grid=None, out_specs=None, unread=0):
    vmem = pl.BlockSpec(memory_space=pltpu.VMEM)
    outs = jax.tree.map(lambda s: jax.ShapeDtypeStruct(s, F32), out_shape, is_leaf=lambda s: isinstance(s[0], int))
    kw = {} if grid is None else {"grid": grid}
    return pl.pallas_call(
        kernel,
        out_shape=outs,
        in_specs=[pl.BlockSpec(memory_space=pltpu.SMEM)] + [vmem] * (len(args) - 1 - unread)
        + [pl.BlockSpec(memory_space=pl.ANY)] * unread,
        out_specs=jax.tree.map(lambda _: vmem, outs) if out_specs is None else out_specs,
        scratch_shapes=list(scratch),
        compiler_params=pltpu.CompilerParams(vmem_limit_bytes=32 * 2**20),
        cost_estimate=pl.CostEstimate(flops=flops, bytes_accessed=4 * 2**20, transcendentals=0),
        **kw,
    )(*args)


def per_device(field, u, v):
    core_id, x_id, zl_id = lax.axis_index("c"), lax.axis_index("x"), lax.axis_index("zl")
    ids = jnp.stack([x_id, core_id, zl_id]).astype(jnp.int32)

    u_half = lax.dynamic_slice_in_dim(u, 128 * core_id, 128, 1)
    send = jnp.concatenate(
        [jnp.transpose(field, (1, 2, 0, 3)), jnp.broadcast_to(u_half, (NY, 1, 128, 128))], axis=1
    )
    own = exchange(send, Y)
    v_all = [v] + [shift(v, "zl", NZL, d) for d in range(1, NZL)]
    own, v_all = lax.optimization_barrier((own, v_all))
    other = lax.ppermute(own, "c", [(0, 1), (1, 0)])

    g1 = call(
        gram_one_kernel,
        (NX, 64, 16, 128),
        2 * 1024 * 512 * 512 * 3,
        ids,
        own,
        other,
        grid=(4,),
        out_specs=pl.BlockSpec((NX, 16, 16, 128), lambda n: (0, n, 0, 0)),
        scratch=[pltpu.VMEM((1024, 512), BF16)] * 2 + [pltpu.VMEM((512, 512), BF16)] * 2,
    )
    z = call(
        project_kernel,
        ((128, 128),) * 4,
        2 * 1024 * 256 * 256 * 3,
        ids,
        own,
        other,
        g1,
        unread=1,
        scratch=[pltpu.VMEM((NZL, 128, 128), F32)],
    )
    z = jnp.stack([z[0]] + [shift(z[d], "zl", NZL, d) for d in range(1, NZL)])

    z_other = lax.ppermute(z, "c", [(0, 1), (1, 0)])
    g2 = call(
        gram_two_kernel,
        ((32, 8, 128),) * 4,
        2 * 512 * 256 * 256 * 3,
        ids,
        z,
        z_other,
        scratch=[pltpu.VMEM((256, 512), BF16)] * 2 + [pltpu.VMEM((512, 256), F32)],
    )
    g2 = [g2[0]] + [shift(g2[d], "x", NX, d) for d in range(1, NX)]
    core = call(core_kernel, (NY, NZL, 8, 128), 2 * 128 * 512 * 512 * 3, ids, z, *v_all)

    g1 = jnp.sum(exchange(g1, "x"), axis=0)
    g2 = jnp.repeat(g2[0] + g2[1] + g2[2] + g2[3], NZH, axis=0)
    core = jnp.repeat(core.reshape(32, 8, 128), NZH, axis=0)
    got = exchange(jnp.concatenate([g1, g2, core], axis=1), Y + ("zl", "zh"))
    g2 = jnp.sum(got[:, 16:24], axis=0)
    g2 = exchange(jnp.broadcast_to(g2, (64, 8, 128)), Y + ("x", "c"))
    gram_one = jnp.transpose(jnp.sum(got[:, :16], axis=0)) / 131072.0
    core = lax.dynamic_index_in_dim(got.reshape(32, NZH, 32, 128), lax.axis_index("zh"), 1, keepdims=False)
    core = core[:, 24:28].reshape(8, 4, 4, 2, 2, 32)
    core = jnp.transpose(core, (1, 4, 2, 0, 3, 5)).reshape(32, 8, 2, 32)
    g2 = g2.reshape(2, NYL, NX, NC, 8, 128)
    g2 = jnp.transpose(g2, (2, 1, 4, 3, 0, 5)).reshape(128, 512)
    gram_two = g2 / 65536.0
    return gram_one, gram_two, core


def solution(mesh):
    by_axis = Mesh(mesh.devices.reshape(2, NYL, NZL, NZH, NX, NC), Y + ("zl", "zh", "x", "c"))
    gz = ("zh", "x", "c")
    return jax.shard_map(
        per_device,
        mesh=by_axis,
        in_specs=(P(Y, None, gz, "zl"), P(Y, None), P("zl", None)),
        out_specs=(P(Y, ("zl",) + gz), P("zl", None), P(Y, None, gz, "zl")),
        check_vma=False,
    )
```

```python
import jax
import jax.numpy as jnp
from jax import lax
from jax.experimental import pallas as pl
from jax.experimental.pallas import tpu as pltpu
from jax.sharding import Mesh
from jax.sharding import PartitionSpec as P

NY, NYL, NZL, NZH, NX, NC = 8, 4, 4, 2, 4, 2
Y = ("yh", "yl")
F32, BF16 = jnp.float32, jnp.bfloat16


def exchange(a, axes):
    return lax.all_to_all(a, axes, 0, 0)


def shift(a, axis, size, d):
    return lax.ppermute(a, axis, [(i, (i + d) % size) for i in range(size)])


def split(a):
    hi = a.astype(BF16)
    return hi, (a - hi.astype(F32)).astype(BF16)


def dot3(a, b, dims):
    def one(p, q):
        return lax.dot_general(p, q, (dims, ((), ())), preferred_element_type=F32)

    return one(a[0], b[0]) + (one(a[0], b[1]) + one(a[1], b[0]))


def project_kernel(ids, own, other, o0, o1, o2, o3, res):
    c = ids[1]
    total = [jnp.zeros((128, 256), F32)] * 2
    for y in range(NY):
        f = split(jnp.concatenate([own[y, 0], own[y, 1]], axis=1))
        for h, ref in enumerate((own, other)):
            total[h] += dot3(split(ref[y, 2]), f, ((0,), (0,)))
    for h in range(2):
        half = c if h == 0 else 1 - c
        for rg in range(4):
            k, first = rg // 2, 4 * (rg % 2)
            at = pl.multiple_of(32 * rg + 16 * half, 16)
            for g in range(4):
                rows = [
                    total[h][32 * yq + 8 * g + first : 32 * yq + 8 * g + first + 4, 128 * k : 128 * k + 128]
                    for yq in range(4)
                ]
                res[g, pl.ds(at, 16), :] = jnp.concatenate(rows, axis=0)
    for d, o in enumerate((o0, o1, o2, o3)):
        o[...] = res[lax.rem(ids[2] + d, NZL)]


def gram_one_kernel(ids, own, other, out, hi, lo, row_hi, row_lo):
    for i, ref in enumerate((own, other)):
        for k in range(2):
            for y in range(NY):
                col = 256 * i + 128 * k
                a, b = split(ref[y, k])
                hi[128 * y : 128 * y + 128, col : col + 128] = a
                lo[128 * y : 128 * y + 128, col : col + 128] = b
    for x in range(NX):
        for b in range(8):
            src = pl.ds(pl.multiple_of(128 * b + 32 * x + 16 * ids[1], 16), 16)
            dst = slice(128 * x + 16 * b, 128 * x + 16 * b + 16)
            row_hi[dst, :] = hi[src, :]
            row_lo[dst, :] = lo[src, :]
    for n in range(4):
        cols = slice(256 * n, 256 * n + 256)
        r = dot3((row_hi[...], row_lo[...]), (hi[cols, :], lo[cols, :]), ((1,), (1,)))
        for x in range(NX):
            for y in range(2):
                for b in range(8):
                    at = 128 * x + 16 * b
                    out[x, 16 * n + 8 * y + b] = r[at : at + 16, 128 * y : 128 * y + 128]


def gram_two_kernel(ids, own, other, o0, o1, o2, o3, hi, lo, res):
    for n, ref in enumerate((own, other)):
        for b in range(4):
            rows = slice(128 * n, 128 * n + 128)
            cols = pl.ds(pl.multiple_of(128 * lax.rem(ids[2] + NZL - b, NZL), 128), 128)
            p, q = split(ref[b])
            hi[rows, cols] = p
            lo[rows, cols] = q
    cols = pl.ds(pl.multiple_of(256 * ids[1], 256), 256)
    res[...] = dot3((hi[...], lo[...]), (hi[:, cols], lo[:, cols]), ((0,), (0,)))
    for d, o in enumerate((o0, o1, o2, o3)):
        x = lax.rem(ids[0] + d, NX)
        for zl in range(NZL):
            part = res[pl.ds(pl.multiple_of(128 * zl + 32 * x, 32), 32), :]
            for yl in range(NYL):
                for lb in range(2):
                    o[NZL * (NYL * lb + yl) + zl] = part[8 * yl : 8 * yl + 8, 128 * lb : 128 * lb + 128]


def core_kernel(ids, z, v0, v1, v2, v3, out):
    lane = lax.broadcasted_iota(jnp.int32, (128, 128), 1)
    total = jnp.zeros((32, 512), F32)
    for n, v in enumerate((v0, v1, v2, v3)):
        zn, vn = z[n], v[...]
        moved = [vn] + [pltpu.roll(vn, 32 * d, 1) for d in range(1, 4)]
        for rg in range(4):
            here = (lane >= 32 * rg) & (lane < 32 * rg + 32)
            cols = [jnp.where(here, moved[(rg - zl) % 4], 0.0) for zl in range(NZL)]
            total += dot3(split(zn[32 * rg : 32 * rg + 32]), split(jnp.concatenate(cols, axis=1)), ((1,), (0,)))
    for y in range(NY):
        for zl in range(NZL):
            part = total[4 * y : 4 * y + 4, 128 * zl : 128 * zl + 128]
            out[y, zl] = jnp.concatenate([part, part], axis=0)


def call(kernel, out_shape, flops, *args, scratch=(), unread=0):
    vmem = pl.BlockSpec(memory_space=pltpu.VMEM)
    outs = jax.tree.map(lambda s: jax.ShapeDtypeStruct(s, F32), out_shape, is_leaf=lambda s: isinstance(s[0], int))
    return pl.pallas_call(
        kernel,
        out_shape=outs,
        in_specs=[pl.BlockSpec(memory_space=pltpu.SMEM)] + [vmem] * (len(args) - 1 - unread)
        + [pl.BlockSpec(memory_space=pl.ANY)] * unread,
        out_specs=jax.tree.map(lambda _: vmem, outs),
        scratch_shapes=list(scratch),
        compiler_params=pltpu.CompilerParams(vmem_limit_bytes=32 * 2**20),
        cost_estimate=pl.CostEstimate(flops=flops, bytes_accessed=4 * 2**20, transcendentals=0),
    )(*args)


def per_device(field, u, v):
    core_id, x_id, zl_id = lax.axis_index("c"), lax.axis_index("x"), lax.axis_index("zl")
    ids = jnp.stack([x_id, core_id, zl_id]).astype(jnp.int32)

    u_half = lax.dynamic_slice_in_dim(u, 128 * core_id, 128, 1)
    send = jnp.concatenate(
        [jnp.transpose(field, (1, 2, 0, 3)), jnp.broadcast_to(u_half, (NY, 1, 128, 128))], axis=1
    )
    own = exchange(send, Y)
    v_all = [v] + [shift(v, "zl", NZL, d) for d in range(1, NZL)]
    own, v_all = lax.optimization_barrier((own, v_all))
    other = lax.ppermute(own, "c", [(0, 1), (1, 0)])

    g1 = call(
        gram_one_kernel,
        (NX, 64, 16, 128),
        2 * 1024 * 512 * 512 * 3,
        ids,
        own,
        other,
        scratch=[pltpu.VMEM((1024, 512), BF16)] * 2 + [pltpu.VMEM((512, 512), BF16)] * 2,
    )
    z = call(
        project_kernel,
        ((128, 128),) * 4,
        2 * 1024 * 256 * 256 * 3,
        ids,
        own,
        other,
        scratch=[pltpu.VMEM((NZL, 128, 128), F32)],
    )
    z = jnp.stack([z[0]] + [shift(z[d], "zl", NZL, d) for d in range(1, NZL)])

    z_other = lax.ppermute(z, "c", [(0, 1), (1, 0)])
    g2 = call(
        gram_two_kernel,
        ((32, 8, 128),) * 4,
        2 * 512 * 256 * 256 * 3,
        ids,
        z,
        z_other,
        scratch=[pltpu.VMEM((256, 512), BF16)] * 2 + [pltpu.VMEM((512, 256), F32)],
    )
    g2 = [g2[0]] + [shift(g2[d], "x", NX, d) for d in range(1, NX)]
    core = call(core_kernel, (NY, NZL, 8, 128), 2 * 128 * 512 * 512 * 3, ids, z, *v_all)

    g1 = jnp.sum(exchange(g1, "x"), axis=0)
    g2 = jnp.repeat(g2[0] + g2[1] + g2[2] + g2[3], NZH, axis=0)
    core = jnp.repeat(core.reshape(32, 8, 128), NZH, axis=0)
    got = exchange(jnp.concatenate([g1, g2, core], axis=1), Y + ("zl", "zh"))
    g2 = jnp.sum(got[:, 16:24], axis=0)
    g2 = exchange(jnp.broadcast_to(g2, (64, 8, 128)), Y + ("x", "c"))
    gram_one = jnp.transpose(jnp.sum(got[:, :16], axis=0)) / 131072.0
    core = lax.dynamic_index_in_dim(got.reshape(32, NZH, 32, 128), lax.axis_index("zh"), 1, keepdims=False)
    core = core[:, 24:28].reshape(8, 4, 4, 2, 2, 32)
    core = jnp.transpose(core, (1, 4, 2, 0, 3, 5)).reshape(32, 8, 2, 32)
    g2 = g2.reshape(2, NYL, NX, NC, 8, 128)
    g2 = jnp.transpose(g2, (2, 1, 4, 3, 0, 5)).reshape(128, 512)
    gram_two = g2 / 65536.0
    return gram_one, gram_two, core


def solution(mesh):
    by_axis = Mesh(mesh.devices.reshape(2, NYL, NZL, NZH, NX, NC), Y + ("zl", "zh", "x", "c"))
    gz = ("zh", "x", "c")
    return jax.shard_map(
        per_device,
        mesh=by_axis,
        in_specs=(P(Y, None, gz, "zl"), P(Y, None), P("zl", None)),
        out_specs=(P(Y, ("zl",) + gz), P("zl", None), P(Y, None, gz, "zl")),
        check_vma=False,
    )
```

```python
import jax
import jax.numpy as jnp
from jax import lax
from jax.experimental import pallas as pl
from jax.experimental.pallas import tpu as pltpu
from jax.sharding import Mesh
from jax.sharding import PartitionSpec as P

NY, NYL, NZL, NZH, NX, NC = 8, 4, 4, 2, 4, 2
Y = ("yh", "yl")
F32, BF16 = jnp.float32, jnp.bfloat16


def exchange(a, axes):
    return lax.all_to_all(a, axes, 0, 0)


def shift(a, axis, size, d):
    return lax.ppermute(a, axis, [(i, (i + d) % size) for i in range(size)])


def split(a):
    hi = a.astype(BF16)
    return hi, (a - hi.astype(F32)).astype(BF16)


def dot3(a, b, dims):
    def one(p, q):
        return lax.dot_general(p, q, (dims, ((), ())), preferred_element_type=F32)

    return one(a[0], b[0]) + (one(a[0], b[1]) + one(a[1], b[0]))


def project_kernel(ids, own, other, o0, o1, o2, o3, res):
    c = ids[1]
    total = [jnp.zeros((128, 256), F32)] * 2
    for y in range(NY):
        f = split(jnp.concatenate([own[y, 0], own[y, 1]], axis=1))
        for h, ref in enumerate((own, other)):
            total[h] += dot3(split(ref[y, 2]), f, ((0,), (0,)))
    for h in range(2):
        half = c if h == 0 else 1 - c
        for rg in range(4):
            k, first = rg // 2, 4 * (rg % 2)
            at = pl.multiple_of(32 * rg + 16 * half, 16)
            for g in range(4):
                rows = [
                    total[h][32 * yq + 8 * g + first : 32 * yq + 8 * g + first + 4, 128 * k : 128 * k + 128]
                    for yq in range(4)
                ]
                res[g, pl.ds(at, 16), :] = jnp.concatenate(rows, axis=0)
    for d, o in enumerate((o0, o1, o2, o3)):
        o[...] = res[lax.rem(ids[2] + d, NZL)]


def gram_one_kernel(ids, own, other, out, hi, lo, row_hi, row_lo):
    for i, ref in enumerate((own, other)):
        for k in range(2):
            for y in range(NY):
                col = 256 * i + 128 * k
                a, b = split(ref[y, k])
                hi[128 * y : 128 * y + 128, col : col + 128] = a
                lo[128 * y : 128 * y + 128, col : col + 128] = b
    for x in range(NX):
        for b in range(8):
            src = pl.ds(pl.multiple_of(128 * b + 32 * x + 16 * ids[1], 16), 16)
            dst = slice(128 * x + 16 * b, 128 * x + 16 * b + 16)
            row_hi[dst, :] = hi[src, :]
            row_lo[dst, :] = lo[src, :]
    for n in range(4):
        cols = slice(256 * n, 256 * n + 256)
        r = dot3((row_hi[...], row_lo[...]), (hi[cols, :], lo[cols, :]), ((1,), (1,)))
        for x in range(NX):
            for y in range(2):
                for b in range(8):
                    at = 128 * x + 16 * b
                    out[x, 16 * n + 8 * y + b] = r[at : at + 16, 128 * y : 128 * y + 128]


def gram_two_kernel(ids, own, other, after, o0, o1, o2, o3, hi, lo, res):
    for n, ref in enumerate((own, other)):
        for b in range(4):
            rows = slice(128 * n, 128 * n + 128)
            cols = pl.ds(pl.multiple_of(128 * lax.rem(ids[2] + NZL - b, NZL), 128), 128)
            p, q = split(ref[b])
            hi[rows, cols] = p
            lo[rows, cols] = q
    cols = pl.ds(pl.multiple_of(256 * ids[1], 256), 256)
    res[...] = dot3((hi[...], lo[...]), (hi[:, cols], lo[:, cols]), ((0,), (0,)))
    for d, o in enumerate((o0, o1, o2, o3)):
        x = lax.rem(ids[0] + d, NX)
        for zl in range(NZL):
            part = res[pl.ds(pl.multiple_of(128 * zl + 32 * x, 32), 32), :]
            for yl in range(NYL):
                for lb in range(2):
                    o[NZL * (NYL * lb + yl) + zl] = part[8 * yl : 8 * yl + 8, 128 * lb : 128 * lb + 128]


def core_kernel(ids, z, v0, v1, v2, v3, out):
    lane = lax.broadcasted_iota(jnp.int32, (128, 128), 1)
    total = jnp.zeros((32, 512), F32)
    for n, v in enumerate((v0, v1, v2, v3)):
        zn, vn = z[n], v[...]
        moved = [vn] + [pltpu.roll(vn, 32 * d, 1) for d in range(1, 4)]
        for rg in range(4):
            here = (lane >= 32 * rg) & (lane < 32 * rg + 32)
            cols = [jnp.where(here, moved[(rg - zl) % 4], 0.0) for zl in range(NZL)]
            total += dot3(split(zn[32 * rg : 32 * rg + 32]), split(jnp.concatenate(cols, axis=1)), ((1,), (0,)))
    for y in range(NY):
        for zl in range(NZL):
            part = total[4 * y : 4 * y + 4, 128 * zl : 128 * zl + 128]
            out[y, zl] = jnp.concatenate([part, part], axis=0)


def call(kernel, out_shape, flops, *args, scratch=(), unread=0):
    vmem = pl.BlockSpec(memory_space=pltpu.VMEM)
    outs = jax.tree.map(lambda s: jax.ShapeDtypeStruct(s, F32), out_shape, is_leaf=lambda s: isinstance(s[0], int))
    return pl.pallas_call(
        kernel,
        out_shape=outs,
        in_specs=[pl.BlockSpec(memory_space=pltpu.SMEM)] + [vmem] * (len(args) - 1 - unread)
        + [pl.BlockSpec(memory_space=pl.ANY)] * unread,
        out_specs=jax.tree.map(lambda _: vmem, outs),
        scratch_shapes=list(scratch),
        compiler_params=pltpu.CompilerParams(vmem_limit_bytes=32 * 2**20),
        cost_estimate=pl.CostEstimate(flops=flops, bytes_accessed=4 * 2**20, transcendentals=0),
    )(*args)


def per_device(field, u, v):
    core_id, x_id, zl_id = lax.axis_index("c"), lax.axis_index("x"), lax.axis_index("zl")
    ids = jnp.stack([x_id, core_id, zl_id]).astype(jnp.int32)

    u_half = lax.dynamic_slice_in_dim(u, 128 * core_id, 128, 1)
    send = jnp.concatenate(
        [jnp.transpose(field, (1, 2, 0, 3)), jnp.broadcast_to(u_half, (NY, 1, 128, 128))], axis=1
    )
    own = exchange(send, Y)
    v_all = [v] + [shift(v, "zl", NZL, d) for d in range(1, NZL)]
    own, v_all = lax.optimization_barrier((own, v_all))
    other = lax.ppermute(own, "c", [(0, 1), (1, 0)])

    g1 = call(
        gram_one_kernel,
        (NX, 64, 16, 128),
        2 * 1024 * 512 * 512 * 3,
        ids,
        own,
        other,
        scratch=[pltpu.VMEM((1024, 512), BF16)] * 2 + [pltpu.VMEM((512, 512), BF16)] * 2,
    )
    z = call(
        project_kernel,
        ((128, 128),) * 4,
        2 * 1024 * 256 * 256 * 3,
        ids,
        own,
        other,
        scratch=[pltpu.VMEM((NZL, 128, 128), F32)],
    )
    z = jnp.stack([z[0]] + [shift(z[d], "zl", NZL, d) for d in range(1, NZL)])

    z_other = lax.ppermute(z, "c", [(0, 1), (1, 0)])
    core = call(core_kernel, (NY, NZL, 8, 128), 2 * 128 * 512 * 512 * 3, ids, z, *v_all)
    g2 = call(
        gram_two_kernel,
        ((32, 8, 128),) * 4,
        2 * 512 * 256 * 256 * 3,
        ids,
        z,
        z_other,
        core,
        unread=1,
        scratch=[pltpu.VMEM((256, 512), BF16)] * 2 + [pltpu.VMEM((512, 256), F32)],
    )
    g2 = [g2[0]] + [shift(g2[d], "x", NX, d) for d in range(1, NX)]

    g1 = jnp.sum(exchange(g1, "x"), axis=0)
    g2 = jnp.repeat(g2[0] + g2[1] + g2[2] + g2[3], NZH, axis=0)
    core = jnp.repeat(core.reshape(32, 8, 128), NZH, axis=0)
    got = exchange(jnp.concatenate([g1, g2, core], axis=1), Y + ("zl", "zh"))
    g2 = jnp.sum(got[:, 16:24], axis=0)
    g2 = exchange(jnp.broadcast_to(g2, (64, 8, 128)), Y + ("x", "c"))
    gram_one = jnp.transpose(jnp.sum(got[:, :16], axis=0)) / 131072.0
    core = lax.dynamic_index_in_dim(got.reshape(32, NZH, 32, 128), lax.axis_index("zh"), 1, keepdims=False)
    core = core[:, 24:28].reshape(8, 4, 4, 2, 2, 32)
    core = jnp.transpose(core, (1, 4, 2, 0, 3, 5)).reshape(32, 8, 2, 32)
    g2 = g2.reshape(2, NYL, NX, NC, 8, 128)
    g2 = jnp.transpose(g2, (2, 1, 4, 3, 0, 5)).reshape(128, 512)
    gram_two = g2 / 65536.0
    return gram_one, gram_two, core


def solution(mesh):
    by_axis = Mesh(mesh.devices.reshape(2, NYL, NZL, NZH, NX, NC), Y + ("zl", "zh", "x", "c"))
    gz = ("zh", "x", "c")
    return jax.shard_map(
        per_device,
        mesh=by_axis,
        in_specs=(P(Y, None, gz, "zl"), P(Y, None), P("zl", None)),
        out_specs=(P(Y, ("zl",) + gz), P("zl", None), P(Y, None, gz, "zl")),
        check_vma=False,
    )
```
